32 devices in a mesh: men: 8 (over y, x, core), women: 4 (over z).
Axes of the slice: x: 2, y: 2, z: 4, core: 2. Of those that a mesh axis runs over, the one named last changes fastest.
Arguments:
- men_embed: bfloat16 [16384, 128], P(('men', 'women')), may hold values from -4 to 4
- women_embed: bfloat16 [4096, 128], P(('women', 'men')), may hold values from -4 to 4
- men_count: int32 [16384], P('men'), may hold values from 1 to 297, as said below
- women_count: int32 [4096], P('women'), may hold values from 1 to 299
- women_root: float32 [4096], P('women'), may hold values from 0.5 to 6, as said below
- men_cotangent: float32 [16384], P('men'), may hold values from -300 to 300
- women_cotangent: float32 [4096], P('women'), may hold values from 24 to 864, as said below
Outputs:
- men_grad: float32 [16384, 128], P(('men', 'women'))
- women_grad: float32 [4096, 128], P(('women', 'men'))
The draws below stay inside these ranges and needn't reach their ends.
Inputs may be any that keep to these rules, and one draw needn't show every extreme that they name: `men_count`: integer masses of the male types. `women_root`: positive. `women_cotangent`: positive.
All inputs are finite; a program needn't handle non-finite values.
Results may differ from the reference program's by a relative error of at most 0.0031.
Values may be sent and summed in bfloat16 or wider, within the bound.
A program may use at most 64 MiB of HBM per device.

```python
import math
import jax
import jax.numpy as jnp
from jax import lax

EMB = 128
MEN = 16384
WOMEN = 4096


def draw_men_count(key, part):
    base_mass = jax.random.randint(key, (MEN,), 1, 100, dtype=jnp.int32)
    levels = 1 + 3 * jnp.arange(MEN, dtype=jnp.int32) // MEN
    return (base_mass * levels).astype(jnp.int32)


def draw_women_root(key, part):
    position = jnp.arange(WOMEN, dtype=jnp.float32) / WOMEN
    rising = 1.0 + 2.0 * position
    base_root = jnp.exp(jax.random.uniform(key, (WOMEN,), jnp.float32, math.log(0.5), math.log(2.0)))
    return (base_root * rising).astype(jnp.float32)


def draw_women_cotangent(key, part):
    position = jnp.arange(WOMEN, dtype=jnp.float32) / WOMEN
    base_cot = jnp.exp(jax.random.uniform(key, (WOMEN,), jnp.float32, math.log(48.0), math.log(192.0)))
    rising = 1.0 + 2.0 * position
    return (base_cot * rising).astype(jnp.float32)


def with_ends(result, own_key, smallest, largest):
    longest = result.shape.index(max(result.shape))
    spots = []
    for shift in (0, 1):
        where = [jax.random.randint(jax.random.fold_in(own_key, axis), (), 0, length) for axis, length in enumerate(result.shape)]
        where[longest] = (where[longest] + shift) % result.shape[longest]
        spots.append(tuple(where))
    return result.at[spots[0]].set(smallest).at[spots[1]].set(largest)


def block_scale(key, dims, shards, least, largest):
    level, own = 1.0, jax.random.fold_in(key, 6)
    for axis_at, parts in shards:
        steps = jnp.exp(jax.random.uniform(jax.random.fold_in(own, axis_at), (parts,), jnp.float32, least / len(shards), largest / len(shards)))
        level = level * jnp.repeat(steps, dims[axis_at] // parts).reshape([-1 if axis == axis_at else 1 for axis in range(len(dims))])
    return level


def scatter_about(own_key, extent, scale, most, split=(), kind=jnp.bfloat16):
    gain = block_scale(own_key, extent, split, -0.22, 0.18) if split else 1.0
    values = jax.random.normal(own_key, extent, jnp.float32) * scale * gain
    return jnp.minimum(jnp.maximum(values, -most), most).astype(kind)


def setup_inputs(seed: int = 0) -> dict:
    seeds = jax.random.split(jax.random.key(seed), 8)
    men_embed = scatter_about(seeds[0], (MEN, EMB), (EMB ** -0.25), 4.0, ((0, 32),))
    women_embed = scatter_about(seeds[1], (WOMEN, EMB), (EMB ** -0.25), 4.0, ((0, 32),))
    men_count = draw_men_count(jax.random.fold_in(seeds[7], 71), 0)
    women_count = with_ends(jax.random.randint(seeds[3], (WOMEN,), 1, 300), jax.random.fold_in(seeds[3], 1), 1, 299).astype(jnp.int32)
    women_root = draw_women_root(jax.random.fold_in(seeds[7], 71), 0)
    men_cotangent = scatter_about(seeds[5], (MEN,), (200.0 * WOMEN / MEN), 300.0, ((0, 8),), jnp.float32)
    women_cotangent = draw_women_cotangent(jax.random.fold_in(seeds[7], 71), 0)
    return dict(men_embed=men_embed, women_embed=women_embed, men_count=men_count, women_count=women_count, women_root=women_root, men_cotangent=men_cotangent, women_cotangent=women_cotangent)


def kernel_rows(men_block, women_full):
    return jnp.exp(0.5 * jnp.dot(men_block, women_full.T, preferred_element_type=jnp.float32))

def round_half(values):
    return lax.optimization_barrier(values.astype(jnp.bfloat16)).astype(jnp.float32)

def reference(men_embed, women_embed, men_count, women_count, women_root, men_cotangent, women_cotangent):
    men_full = men_embed.astype(jnp.float32)
    women_full = women_embed.astype(jnp.float32)
    men_mass = men_count.astype(jnp.float32)
    women_mass = women_count.astype(jnp.float32)
    row_total = men_full.shape[0]
    block_rows = math.gcd(row_total, 2048)
    block_number = row_total // block_rows
    men_blocks = men_full.reshape(block_number, block_rows, EMB)
    mass_blocks = men_mass.reshape(block_number, block_rows)
    cot_blocks = men_cotangent.reshape(block_number, block_rows)

    def first_pass(column_total, pieces):
        men_block, mass_block = pieces
        kernel = kernel_rows(men_block, women_full)
        weighted = kernel * women_root[None, :]
        row_mass = lax.optimization_barrier(jnp.sum(weighted, axis=1))
        disc_rows = jnp.sqrt(row_mass * row_mass + 4.0 * mass_block)
        root_rows = 2.0 * mass_block / (row_mass + disc_rows)
        product = jnp.dot(round_half(weighted), women_full, preferred_element_type=jnp.float32)
        column_total = column_total + lax.optimization_barrier(jnp.sum(kernel * root_rows[:, None], axis=0))
        return (column_total, (root_rows, disc_rows, product))
    col_mass, (men_root, men_disc, weighted_v) = lax.scan(first_pass, jnp.zeros((women_full.shape[0],), jnp.float32), (men_blocks, mass_blocks))
    women_disc = jnp.sqrt(col_mass * col_mass + 4.0 * women_mass)
    col_grad = -women_cotangent / women_disc

    def second_pass(women_total, pieces):
        men_block, root_rows, disc_rows, product, cot_rows = pieces
        kernel = kernel_rows(men_block, women_full)
        weighted = kernel * col_grad[None, :]
        row_cot = lax.optimization_barrier(jnp.sum(weighted, axis=1))
        direct = jnp.dot(round_half(weighted), women_full, preferred_element_type=jnp.float32)
        row_grad = -(cot_rows + root_rows * row_cot) / disc_rows
        men_part = 0.5 * (row_grad[:, None] * product + root_rows[:, None] * direct)
        tangent = round_half(0.5 * kernel * (row_grad[:, None] * women_root[None, :] + root_rows[:, None] * col_grad[None, :]))
        women_total = women_total + jnp.dot(tangent.T, men_block, preferred_element_type=jnp.float32)
        return (women_total, men_part)
    women_grad, men_parts = lax.scan(second_pass, jnp.zeros((women_full.shape[0], EMB), jnp.float32), (men_blocks, men_root, men_disc, weighted_v, cot_blocks))
    return (men_parts.reshape(row_total, EMB), women_grad)
```

```python
import functools
import math

import jax
import jax.numpy as jnp
from jax import lax
from jax.experimental import pallas as pl
from jax.experimental.pallas import tpu as pltpu
from jax.sharding import PartitionSpec as P

F32 = jnp.float32
BF16 = jnp.bfloat16
MESH = pl.DeviceIdType.MESH
HALF_LOG2E = 0.5 * math.log2(math.e)


def loop(start, stop, step_fn):
    if stop - start <= 8:
        for i in range(start, stop):
            step_fn(i)
    else:
        lax.fori_loop(start, stop, lambda i, _: (step_fn(i), 0)[1], 0)


def kernel(
    n_men, n_women,
    men_ref, women_ref, count_ref, cot_ref, root_ref, wcount_ref, wcot_ref,
    men_out, women_out,
    wbuf, kmat, rootbuf, gradbuf, rootg, gradg, colp, pieces, zsum, psum_, quarter,
    wv, dv, rsum, tang, csend, crecv, keep, xsend, xrecv, zsend, zrecv,
    ag_recv, ag_zsend, ag_xsend, ag_csend,
    root_send, root_recv, cz_send, cz_recv, cp_send, cp_recv, cg_send, cg_recv,
    gc_send, gc_recv, gx_send, gx_recv, gz_send, gz_recv,
):
    rows = men_ref.shape[0]
    width = women_ref.shape[0]
    group = n_women * width
    n_chips = n_men // 2
    chunk = min(rows, 128)
    m = lax.axis_index("men")
    w = lax.axis_index("women")
    c = m // 2
    core = m % 2
    sib = c * 2 + (1 - core)

    def z_to(j):
        return lax.rem(w + j, n_women)

    def z_from(j):
        return lax.rem(w + n_women - j, n_women)

    def chip_to(k):
        return lax.rem(c + k, n_chips)

    def chip_from(k):
        return lax.rem(c + n_chips - k, n_chips)

    def copy(src, dst, send, recv, to_m, to_w):
        return pltpu.make_async_remote_copy(
            src_ref=src, dst_ref=dst, send_sem=send, recv_sem=recv,
            device_id=(to_m, to_w), device_id_type=MESH,
        )

    barrier = pltpu.get_barrier_semaphore()
    loop(1, n_women, lambda j: pl.semaphore_signal(
        barrier, inc=1, device_id=(m, z_to(j)), device_id_type=MESH))
    loop(1, n_men, lambda j: pl.semaphore_signal(
        barrier, inc=1, device_id=(lax.rem(m + j, n_men), w), device_id_type=MESH))
    wbuf[m, w] = women_ref[...]
    rootbuf[w] = root_ref[...]
    pl.semaphore_wait(barrier, n_women + n_men - 2)

    def block_copy(at_m, at_w, send, to_m, to_w):
        return copy(wbuf.at[at_m, at_w], wbuf.at[at_m, at_w], send,
                    ag_recv.at[at_m, at_w], to_m, to_w)

    def z_copy(j):
        return block_copy(m, w, ag_zsend.at[j], m, z_to(j))

    def x_copy(k, j):
        return block_copy(m, z_from(j), ag_xsend.at[k, j], chip_to(k) * 2 + core, w)

    def c_copy(k, j):
        return block_copy(chip_from(k) * 2 + core, z_from(j), ag_csend.at[k, j], sib, w)

    def landed(at_m, at_w):
        block_copy(at_m, at_w, ag_zsend.at[0], sib, w).wait_recv()

    def root_copy(j):
        return copy(rootbuf.at[w], rootbuf.at[w], root_send.at[j], root_recv.at[j], m, z_to(j))

    loop(1, n_women, lambda j: z_copy(j).start())
    loop(1, n_chips, lambda k: x_copy(k, 0).start())
    loop(1, n_women, lambda j: root_copy(j).start())
    c_copy(0, 0).start()

    def column(row):
        return jnp.broadcast_to(row, (128, rows)).T

    mass = column(count_ref[w].astype(F32))
    men_cot = column(cot_ref[w])
    men_t = men_ref[...].astype(F32).T.astype(BF16)
    rsum[...] = jnp.zeros_like(rsum)
    wv[...] = jnp.zeros_like(wv)

    def pass_on(j):
        landed(m, z_from(j))
        loop(1, n_chips, lambda k: x_copy(k, j).start())
        c_copy(0, j).start()

    loop(1, n_women, pass_on)
    loop(1, n_women, lambda j: root_copy(j).wait_recv())

    def spread(buf, out):
        for i in range(n_women):
            out[:, i * width:(i + 1) * width] = buf[i]

    spread(rootbuf, rootg)

    def lanes(values):
        total = values[:, :128]
        for i in range(1, group // 128):
            total = total + values[:, i * 128:(i + 1) * 128]
        return total

    def first(g):
        block = wbuf[g].reshape(group, 128)
        roots = rootg[pl.ds(g, 1), :]
        for r in range(0, rows, chunk):
            at = pl.ds(r, chunk)
            phi = lax.dot_general(men_ref[at, :], block, (((1,), (1,)), ((), ())),
                                  preferred_element_type=F32)
            k = jnp.exp2(phi * HALF_LOG2E)
            kmat[g, at, :] = k
            weighted = k * roots
            rsum[at, :] += lanes(weighted)
            wv[at, :] += jnp.dot(weighted.astype(BF16), block, preferred_element_type=F32)

    def all_landed(at_m):
        loop(0, n_women, lambda i: landed(at_m, i))

    def from_chip(k):
        at_m = chip_from(k) * 2 + core

        def forward(j):
            landed(at_m, z_from(j))
            c_copy(k, j).start()

        loop(0, n_women, forward)
        first(at_m)

    def from_sibling(k):
        at_m = chip_from(k) * 2 + (1 - core)
        all_landed(at_m)
        first(at_m)

    first(m)
    from_sibling(0)
    loop(1, n_chips, from_chip)
    loop(1, n_chips, from_sibling)

    row_mass = jnp.broadcast_to(jnp.sum(rsum[...], axis=1, keepdims=True), (rows, 128))
    men_disc = jnp.sqrt(row_mass * row_mass + 4.0 * mass)
    men_root = 2.0 * mass / (row_mass + men_disc)

    def wide(values):
        return jnp.concatenate([values] * (group // 128), axis=1)

    def second(g):
        total = jnp.zeros((8, group), F32)
        for r in range(0, rows, chunk):
            term = kmat[g, pl.ds(r, chunk), :] * wide(men_root[r:r + chunk])
            total = total + jnp.sum(term.reshape(chunk // 8, 8, group), axis=0)
        colp[pl.ds(g, 1), :] = jnp.sum(total, axis=0, keepdims=True)

    loop(0, n_men, second)

    for i in range(n_women):
        pieces[i] = colp[:, i * width:(i + 1) * width]

    def cz_copy(j):
        return copy(pieces.at[z_to(j)], zsum.at[j], cz_send.at[j], cz_recv.at[j], m, z_to(j))

    loop(1, n_women, lambda j: cz_copy(j).start())
    quarter[...] = pieces[w]

    def add_z(j):
        cz_copy(j).wait_recv()
        quarter[...] += zsum[j]

    loop(1, n_women, add_z)

    def cp_copy(j):
        return copy(quarter, psum_.at[j], cp_send.at[j], cp_recv.at[j],
                    lax.rem(m + j, n_men), w)

    loop(1, n_men, lambda j: cp_copy(j).start())
    psum_[0] = quarter[...]

    def add_p(j):
        cp_copy(j).wait_recv()
        psum_[0] += psum_[j]

    loop(1, n_men, add_p)
    col_mass = psum_[0]
    women_disc = jnp.sqrt(col_mass * col_mass + 4.0 * wcount_ref[...].astype(F32))
    gradbuf[w] = -wcot_ref[...] / women_disc

    def cg_copy(j):
        return copy(gradbuf.at[w], gradbuf.at[w], cg_send.at[j], cg_recv.at[j], m, z_to(j))

    loop(1, n_women, lambda j: cg_copy(j).start())
    rsum[...] = jnp.zeros_like(rsum)
    dv[...] = jnp.zeros_like(dv)
    loop(1, n_women, lambda j: cg_copy(j).wait_recv())
    spread(gradbuf, gradg)

    def third(g):
        block = wbuf[g].reshape(group, 128)
        grads = gradg[pl.ds(g, 1), :]
        for r in range(0, rows, chunk):
            at = pl.ds(r, chunk)
            weighted = kmat[g, at, :] * grads
            rsum[at, :] += lanes(weighted)
            dv[at, :] += jnp.dot(weighted.astype(BF16), block, preferred_element_type=F32)

    loop(0, n_men, third)
    row_cot = jnp.broadcast_to(jnp.sum(rsum[...], axis=1, keepdims=True), (rows, 128))
    row_grad = -(men_cot + men_root * row_cot) / men_disc
    half_grad = 0.5 * row_grad
    half_root = 0.5 * men_root
    men_out[...] = half_grad * wv[...] + half_root * dv[...]

    def fourth(g):
        roots = rootg[pl.ds(g, 1), :]
        grads = gradg[pl.ds(g, 1), :]
        for r in range(0, rows, chunk):
            at = pl.ds(r, chunk)
            scale = wide(half_grad[r:r + chunk]) * roots + wide(half_root[r:r + chunk]) * grads
            tang[at, :] = (kmat[g, at, :] * scale).astype(BF16)
        return jnp.dot(men_t, tang[...], preferred_element_type=F32).T

    def gc_copy(k):
        return copy(csend.at[k], crecv.at[k], gc_send.at[k], gc_recv.at[k], sib, w)

    def gx_copy(k):
        return copy(xsend.at[k], xrecv.at[k], gx_send.at[k], gx_recv.at[k],
                    chip_to(k) * 2 + core, w)

    def gz_copy(j):
        return copy(zsend.at[z_to(j)], zrecv.at[j], gz_send.at[j], gz_recv.at[j], m, z_to(j))

    def chip_terms(k):
        csend[k] = fourth(chip_to(k) * 2 + (1 - core))
        gc_copy(k).start()
        keep[...] = fourth(chip_to(k) * 2 + core)
        gc_copy(k).wait_recv()

    def to_chip(k):
        chip_terms(k)
        xsend[k] = (keep[...] + crecv[k]).astype(BF16)
        gx_copy(k).start()

    loop(1, n_chips, to_chip)
    chip_terms(0)
    keep[...] += crecv[0]

    def add_x(k):
        gx_copy(k).wait_recv()
        keep[...] += xrecv[k].astype(F32)

    loop(1, n_chips, add_x)
    zsend[...] = keep[...].reshape(n_women, width, 128).astype(BF16)
    loop(1, n_women, lambda j: gz_copy(j).start())
    women_out[...] = keep[pl.ds(pl.multiple_of(w * width, width), width), :]

    def add_grad(j):
        gz_copy(j).wait_recv()
        women_out[...] += zrecv[j].astype(F32)

    loop(1, n_women, add_grad)

    def z_sends(j):
        z_copy(j).wait_send()
        root_copy(j).wait_send()
        cz_copy(j).wait_send()
        cg_copy(j).wait_send()
        gz_copy(j).wait_send()

    loop(1, n_women, z_sends)
    loop(1, n_men, lambda j: cp_copy(j).wait_send())
    loop(0, n_women, lambda j: loop(1, n_chips, lambda k: x_copy(k, j).wait_send()))
    loop(0, n_women, lambda j: loop(0, n_chips, lambda k: c_copy(k, j).wait_send()))
    loop(0, n_chips, lambda k: gc_copy(k).wait_send())
    loop(1, n_chips, lambda k: gx_copy(k).wait_send())


def body(
    n_men, n_women,
    men_embed, women_embed, men_count, women_count, women_root, men_cotangent, women_cotangent
):
    rows, emb = men_embed.shape
    width = women_embed.shape[0]
    group = n_women * width
    n_chips = n_men // 2
    dma = pltpu.SemaphoreType.DMA
    vmem = pl.BlockSpec(memory_space=pltpu.VMEM)
    quarter = (n_men, width)
    return pl.pallas_call(
        functools.partial(kernel, n_men, n_women),
        out_shape=(
            jax.ShapeDtypeStruct((rows, emb), F32),
            jax.ShapeDtypeStruct((width, emb), F32),
        ),
        in_specs=[vmem] * 7,
        out_specs=(vmem, vmem),
        scratch_shapes=[
            pltpu.VMEM((n_men, n_women, width, emb), BF16),
            pltpu.VMEM((n_men, rows, group), F32),
            pltpu.VMEM((n_women,) + quarter, F32),
            pltpu.VMEM((n_women,) + quarter, F32),
            pltpu.VMEM((n_men, group), F32),
            pltpu.VMEM((n_men, group), F32),
            pltpu.VMEM((n_men, group), F32),
            pltpu.VMEM((n_women,) + quarter, F32),
            pltpu.VMEM((n_women,) + quarter, F32),
            pltpu.VMEM((n_men,) + quarter, F32),
            pltpu.VMEM(quarter, F32),
            pltpu.VMEM((rows, emb), F32),
            pltpu.VMEM((rows, emb), F32),
            pltpu.VMEM((rows, 128), F32),
            pltpu.VMEM((rows, group), BF16),
            pltpu.VMEM((n_chips, group, emb), F32),
            pltpu.VMEM((n_chips, group, emb), F32),
            pltpu.VMEM((group, emb), F32),
            pltpu.VMEM((n_chips, group, emb), BF16),
            pltpu.VMEM((n_chips, group, emb), BF16),
            pltpu.VMEM((n_women, width, emb), BF16),
            pltpu.VMEM((n_women, width, emb), BF16),
            dma((n_men, n_women)),
            dma((n_women,)),
            dma((n_chips, n_women)),
            dma((n_chips, n_women)),
            dma((n_women,)), dma((n_women,)),
            dma((n_women,)), dma((n_women,)),
            dma((n_men,)), dma((n_men,)),
            dma((n_women,)), dma((n_women,)),
            dma((n_chips,)), dma((n_chips,)),
            dma((n_chips,)), dma((n_chips,)),
            dma((n_women,)), dma((n_women,)),
        ],
        compiler_params=pltpu.CompilerParams(
            collective_id=0, has_side_effects=True, vmem_limit_bytes=48 * 1024 * 1024,
        ),
        name="matching_backward",
    )(
        men_embed, women_embed,
        men_count.reshape(n_women, 1, rows), men_cotangent.reshape(n_women, 1, rows),
        women_root.reshape(quarter), women_count.reshape(quarter),
        women_cotangent.reshape(quarter),
    )


def solution(mesh):
    return jax.shard_map(
        functools.partial(body, mesh.shape["men"], mesh.shape["women"]),
        mesh=mesh,
        in_specs=(
            P(("men", "women"), None),
            P(("women", "men"), None),
            P("men"),
            P("women"),
            P("women"),
            P("men"),
            P("women"),
        ),
        out_specs=(P(("men", "women"), None), P(("women", "men"), None)),
        check_vma=False,
    )
```

```python
import functools
import math

import jax
import jax.numpy as jnp
from jax import lax
from jax.experimental import pallas as pl
from jax.experimental.pallas import tpu as pltpu
from jax.sharding import PartitionSpec as P

F32 = jnp.float32
BF16 = jnp.bfloat16
MESH = pl.DeviceIdType.MESH
HALF_LOG2E = 0.5 * math.log2(math.e)


def loop(start, stop, step_fn):
    if stop - start <= 8:
        for i in range(start, stop):
            step_fn(i)
    else:
        lax.fori_loop(start, stop, lambda i, _: (step_fn(i), 0)[1], 0)


def kernel(
    n_men, n_women,
    men_hbm, women_hbm, count_hbm, cot_hbm, root_hbm, wcount_hbm, wcot_hbm,
    men_out, women_out,
    men_ref, count_ref, cot_ref, wbuf, kmat, rootbuf, wcountbuf, wcotbuf,
    rootg, wcountg, wcotg, gradg, colp, colrecv, zpart,
    wv, dv, rsum, tang, csend, crecv, keep, xsend, xrecv, zsend, zrecv,
    local, ag_recv, ag_zsend, ag_xsend, ag_csend,
    root_send, root_recv, cz_send, cz_recv, cp_send, cp_recv, cg_send, cg_recv,
    gc_send, gc_recv, gx_send, gx_recv, gz_send, gz_recv,
):
    rows = men_hbm.shape[0]
    width = women_hbm.shape[0]
    group = n_women * width
    n_chips = n_men // 2
    chunk = min(rows, 128)
    m = lax.axis_index("men")
    w = lax.axis_index("women")
    c = m // 2
    core = m % 2
    sib = c * 2 + (1 - core)

    def z_to(j):
        return lax.rem(w + j, n_women)

    def z_from(j):
        return lax.rem(w + n_women - j, n_women)

    def chip_to(k):
        return lax.rem(c + k, n_chips)

    def chip_from(k):
        return lax.rem(c + n_chips - k, n_chips)

    def copy(src, dst, send, recv, to_m, to_w):
        return pltpu.make_async_remote_copy(
            src_ref=src, dst_ref=dst, send_sem=send, recv_sem=recv,
            device_id=(to_m, to_w), device_id_type=MESH,
        )

    fetches = [
        pltpu.make_async_copy(src, dst, local.at[i])
        for i, (src, dst) in enumerate((
            (women_hbm, wbuf.at[m, w]), (root_hbm, rootbuf.at[w]),
            (wcount_hbm, wcountbuf.at[w]), (wcot_hbm, wcotbuf.at[w]),
            (men_hbm, men_ref), (count_hbm.at[w], count_ref), (cot_hbm.at[w], cot_ref),
        ))
    ]
    for fetch in fetches:
        fetch.start()

    barrier = pltpu.get_barrier_semaphore()
    loop(1, n_women, lambda j: pl.semaphore_signal(
        barrier, inc=1, device_id=(m, z_to(j)), device_id_type=MESH))
    loop(1, n_men, lambda j: pl.semaphore_signal(
        barrier, inc=1, device_id=(lax.rem(m + j, n_men), w), device_id_type=MESH))
    fetches[0].wait()
    pl.semaphore_wait(barrier, n_women + n_men - 2)

    def block_copy(at_m, at_w, send, to_m, to_w):
        return copy(wbuf.at[at_m, at_w], wbuf.at[at_m, at_w], send,
                    ag_recv.at[at_m, at_w], to_m, to_w)

    def z_copy(j):
        return block_copy(m, w, ag_zsend.at[j], m, z_to(j))

    def x_copy(k, j):
        return block_copy(m, z_from(j), ag_xsend.at[k, j], chip_to(k) * 2 + core, w)

    def c_copy(k, j):
        return block_copy(chip_from(k) * 2 + core, z_from(j), ag_csend.at[k, j], sib, w)

    def landed(at_m, at_w):
        block_copy(at_m, at_w, ag_zsend.at[0], sib, w).wait_recv()

    def vector_copies(j):
        return [copy(buf.at[w], buf.at[w], root_send.at[i, j], root_recv.at[i, j], m, z_to(j))
                for i, buf in enumerate((rootbuf, wcountbuf, wcotbuf))]

    def each(copies, act):
        for one in copies:
            getattr(one, act)()

    loop(1, n_women, lambda j: z_copy(j).start())
    loop(1, n_chips, lambda k: x_copy(k, 0).start())
    c_copy(0, 0).start()
    for fetch in fetches[1:]:
        fetch.wait()
    loop(1, n_women, lambda j: each(vector_copies(j), "start"))

    def column(row):
        return jnp.broadcast_to(row, (128, rows)).T

    mass = column(count_ref[...].astype(F32))
    men_cot = column(cot_ref[...])
    men_t = men_ref[...].astype(F32).T.astype(BF16)
    rsum[...] = jnp.zeros_like(rsum)
    wv[...] = jnp.zeros_like(wv)

    def pass_on(j):
        landed(m, z_from(j))
        loop(1, n_chips, lambda k: x_copy(k, j).start())
        c_copy(0, j).start()

    loop(1, n_women, pass_on)
    loop(1, n_women, lambda j: each(vector_copies(j), "wait_recv"))

    def spread(buf, out):
        for i in range(n_women):
            out[:, i * width:(i + 1) * width] = buf[i]

    spread(rootbuf, rootg)
    spread(wcountbuf, wcountg)
    spread(wcotbuf, wcotg)

    def lanes(values):
        total = values[:, :128]
        for i in range(1, group // 128):
            total = total + values[:, i * 128:(i + 1) * 128]
        return total

    def first(g):
        block = wbuf[g].reshape(group, 128)
        roots = rootg[pl.ds(g, 1), :]
        for r in range(0, rows, chunk):
            at = pl.ds(r, chunk)
            phi = lax.dot_general(men_ref[at, :], block, (((1,), (1,)), ((), ())),
                                  preferred_element_type=F32)
            k = jnp.exp2(phi * HALF_LOG2E)
            kmat[g, at, :] = k
            weighted = k * roots
            rsum[at, :] += lanes(weighted)
            wv[at, :] += jnp.dot(weighted.astype(BF16), block, preferred_element_type=F32)

    def all_landed(at_m):
        loop(0, n_women, lambda i: landed(at_m, i))

    def from_chip(k):
        at_m = chip_from(k) * 2 + core

        def forward(j):
            landed(at_m, z_from(j))
            c_copy(k, j).start()

        loop(0, n_women, forward)
        first(at_m)

    def from_sibling(k):
        at_m = chip_from(k) * 2 + (1 - core)
        all_landed(at_m)
        first(at_m)

    first(m)
    from_sibling(0)
    loop(1, n_chips, from_chip)
    loop(1, n_chips, from_sibling)

    row_mass = jnp.broadcast_to(jnp.sum(rsum[...], axis=1, keepdims=True), (rows, 128))
    men_disc = jnp.sqrt(row_mass * row_mass + 4.0 * mass)
    men_root = 2.0 * mass / (row_mass + men_disc)

    def wide(values):
        return jnp.concatenate([values] * (group // 128), axis=1)

    def second(g):
        total = jnp.zeros((8, group), F32)
        for r in range(0, rows, chunk):
            term = kmat[g, pl.ds(r, chunk), :] * wide(men_root[r:r + chunk])
            total = total + jnp.sum(term.reshape(chunk // 8, 8, group), axis=0)
        colp[g] = jnp.sum(total, axis=0, keepdims=True)

    def near(j):
        return lax.rem(m + j, n_men)

    def cp_copy(j):
        return copy(colp.at[near(j)], colrecv.at[j], cp_send.at[j], cp_recv.at[j], near(j), w)

    def cz_copy(j):
        return copy(zpart.at[0], zpart.at[j], cz_send.at[j], cz_recv.at[j], m, z_to(j))

    def cg_copy(j):
        return copy(gradg.at[m], gradg.at[m], cg_send.at[j], cg_recv.at[j], near(j), w)

    def for_owner(j):
        second(near(j))
        cp_copy(j).start()

    loop(1, n_men, for_owner)
    second(m)
    zpart[0] = colp[m]
    rsum[...] = jnp.zeros_like(rsum)
    dv[...] = jnp.zeros_like(dv)

    def add_p(j):
        cp_copy(j).wait_recv()
        zpart[0] += colrecv[j]

    loop(1, n_men, add_p)
    loop(1, n_women, lambda j: cz_copy(j).start())
    colp[m] = zpart[0]

    def add_z(j):
        cz_copy(j).wait_recv()
        colp[m] += zpart[j]

    loop(1, n_women, add_z)
    col_mass = colp[m]
    women_mass = wcountg[pl.ds(m, 1), :].astype(F32)
    women_disc = jnp.sqrt(col_mass * col_mass + 4.0 * women_mass)
    gradg[m] = -wcotg[pl.ds(m, 1), :] / women_disc
    loop(1, n_men, lambda j: cg_copy(j).start())

    def third(g):
        block = wbuf[g].reshape(group, 128)
        grads = gradg[g]
        for r in range(0, rows, chunk):
            at = pl.ds(r, chunk)
            weighted = kmat[g, at, :] * grads
            rsum[at, :] += lanes(weighted)
            dv[at, :] += jnp.dot(weighted.astype(BF16), block, preferred_element_type=F32)

    def third_from(j):
        cg_copy(j).wait_recv()
        third(lax.rem(m + n_men - j, n_men))

    third(m)
    loop(1, n_men, third_from)
    row_cot = jnp.broadcast_to(jnp.sum(rsum[...], axis=1, keepdims=True), (rows, 128))
    row_grad = -(men_cot + men_root * row_cot) / men_disc
    half_grad = 0.5 * row_grad
    half_root = 0.5 * men_root
    men_out[...] = half_grad * wv[...] + half_root * dv[...]

    def fourth(g):
        roots = rootg[pl.ds(g, 1), :]
        grads = gradg[g]
        for r in range(0, rows, chunk):
            at = pl.ds(r, chunk)
            scale = wide(half_grad[r:r + chunk]) * roots + wide(half_root[r:r + chunk]) * grads
            tang[at, :] = (kmat[g, at, :] * scale).astype(BF16)
        return jnp.dot(men_t, tang[...], preferred_element_type=F32).T

    def gc_copy(k):
        return copy(csend.at[k], crecv.at[k], gc_send.at[k], gc_recv.at[k], sib, w)

    def gx_copy(k, j):
        return copy(xsend.at[k, z_to(j)], xrecv.at[k, z_to(j)], gx_send.at[k, j],
                    gx_recv.at[k, j], chip_to(k) * 2 + core, w)

    def gz_copy(j):
        return copy(zsend.at[j], zrecv.at[j], gz_send.at[j], gz_recv.at[j], m, z_to(j))

    def chip_terms(k):
        csend[k] = fourth(chip_to(k) * 2 + (1 - core))
        gc_copy(k).start()
        keep[...] = fourth(chip_to(k) * 2 + core)
        gc_copy(k).wait_recv()

    def to_chip(k):
        chip_terms(k)
        xsend[k] = (keep[...] + crecv[k]).reshape(n_women, width, 128).astype(BF16)
        loop(1, n_women, lambda j: gx_copy(k, j).start())
        gx_copy(k, 0).start()

    loop(1, n_chips, to_chip)
    chip_terms(0)
    keep[...] += crecv[0]

    def part(j):
        return keep.at[pl.ds(pl.multiple_of(z_to(j) * width, width), width), :]

    def add_x(j):
        loop(1, n_chips, lambda k: gx_copy(k, j).wait_recv())
        total = part(j)[...]
        for k in range(1, n_chips):
            total = total + xrecv[k, z_to(j)].astype(F32)
        return total

    def along_z(j):
        zsend[j] = add_x(j).astype(BF16)
        gz_copy(j).start()

    loop(1, n_women, along_z)
    women_out[...] = add_x(0)

    def add_grad(j):
        gz_copy(j).wait_recv()
        women_out[...] += zrecv[j].astype(F32)

    loop(1, n_women, add_grad)

    def z_sends(j):
        z_copy(j).wait_send()
        each(vector_copies(j), "wait_send")
        cz_copy(j).wait_send()
        gz_copy(j).wait_send()

    loop(1, n_women, z_sends)
    loop(1, n_men, lambda j: cp_copy(j).wait_send())
    loop(1, n_men, lambda j: cg_copy(j).wait_send())
    loop(0, n_women, lambda j: loop(1, n_chips, lambda k: x_copy(k, j).wait_send()))
    loop(0, n_women, lambda j: loop(0, n_chips, lambda k: c_copy(k, j).wait_send()))
    loop(0, n_chips, lambda k: gc_copy(k).wait_send())
    loop(0, n_women, lambda j: loop(1, n_chips, lambda k: gx_copy(k, j).wait_send()))


def body(
    n_men, n_women,
    men_embed, women_embed, men_count, women_count, women_root, men_cotangent, women_cotangent
):
    rows, emb = men_embed.shape
    width = women_embed.shape[0]
    group = n_women * width
    n_chips = n_men // 2
    dma = pltpu.SemaphoreType.DMA
    vmem = pl.BlockSpec(memory_space=pltpu.VMEM)
    quarter = (n_men, width)
    return pl.pallas_call(
        functools.partial(kernel, n_men, n_women),
        out_shape=(
            jax.ShapeDtypeStruct((rows, emb), F32),
            jax.ShapeDtypeStruct((width, emb), F32),
        ),
        in_specs=[pl.BlockSpec(memory_space=pltpu.HBM)] * 7,
        out_specs=(vmem, vmem),
        scratch_shapes=[
            pltpu.VMEM((rows, emb), BF16),
            pltpu.VMEM((1, rows), jnp.int32),
            pltpu.VMEM((1, rows), F32),
            pltpu.VMEM((n_men, n_women, width, emb), BF16),
            pltpu.VMEM((n_men, rows, group), F32),
            pltpu.VMEM((n_women,) + quarter, F32),
            pltpu.VMEM((n_women,) + quarter, jnp.int32),
            pltpu.VMEM((n_women,) + quarter, F32),
            pltpu.VMEM((n_men, group), F32),
            pltpu.VMEM((n_men, group), jnp.int32),
            pltpu.VMEM((n_men, group), F32),
            pltpu.VMEM((n_men, 1, group), F32),
            pltpu.VMEM((n_men, 1, group), F32),
            pltpu.VMEM((n_men, 1, group), F32),
            pltpu.VMEM((n_women, 1, group), F32),
            pltpu.VMEM((rows, emb), F32),
            pltpu.VMEM((rows, emb), F32),
            pltpu.VMEM((rows, 128), F32),
            pltpu.VMEM((rows, group), BF16),
            pltpu.VMEM((n_chips, group, emb), F32),
            pltpu.VMEM((n_chips, group, emb), F32),
            pltpu.VMEM((group, emb), F32),
            pltpu.VMEM((n_chips, n_women, width, emb), BF16),
            pltpu.VMEM((n_chips, n_women, width, emb), BF16),
            pltpu.VMEM((n_women, width, emb), BF16),
            pltpu.VMEM((n_women, width, emb), BF16),
            dma((7,)),
            dma((n_men, n_women)),
            dma((n_women,)),
            dma((n_chips, n_women)),
            dma((n_chips, n_women)),
            dma((3, n_women)), dma((3, n_women)),
            dma((n_women,)), dma((n_women,)),
            dma((n_men,)), dma((n_men,)),
            dma((n_men,)), dma((n_men,)),
            dma((n_chips,)), dma((n_chips,)),
            dma((n_chips, n_women)), dma((n_chips, n_women)),
            dma((n_women,)), dma((n_women,)),
        ],
        compiler_params=pltpu.CompilerParams(
            collective_id=0, has_side_effects=True, vmem_limit_bytes=48 * 1024 * 1024,
        ),
        name="matching_backward",
    )(
        men_embed, women_embed,
        men_count.reshape(n_women, 1, rows), men_cotangent.reshape(n_women, 1, rows),
        women_root.reshape(quarter), women_count.reshape(quarter),
        women_cotangent.reshape(quarter),
    )


def solution(mesh):
    return jax.shard_map(
        functools.partial(body, mesh.shape["men"], mesh.shape["women"]),
        mesh=mesh,
        in_specs=(
            P(("men", "women"), None),
            P(("women", "men"), None),
            P("men"),
            P("women"),
            P("women"),
            P("men"),
            P("women"),
        ),
        out_specs=(P(("men", "women"), None), P(("women", "men"), None)),
        check_vma=False,
    )
```

```python
import functools
import math

import jax
import jax.numpy as jnp
from jax import lax
from jax.experimental import pallas as pl
from jax.experimental.pallas import tpu as pltpu
from jax.sharding import PartitionSpec as P

F32 = jnp.float32
BF16 = jnp.bfloat16
MESH = pl.DeviceIdType.MESH
HALF_LOG2E = 0.5 * math.log2(math.e)


def loop(start, stop, step_fn):
    if stop - start <= 8:
        for i in range(start, stop):
            step_fn(i)
    else:
        lax.fori_loop(start, stop, lambda i, _: (step_fn(i), 0)[1], 0)


def kernel(
    n_men, n_women,
    men_hbm, women_hbm, count_hbm, cot_hbm, root_hbm, wcount_hbm, wcot_hbm,
    men_out, women_out,
    men_ref, count_ref, cot_ref, wbuf, kmat, rootbuf, wcountbuf, wcotbuf,
    rootg, wcountg, wcotg, gradg, colp, colrecv, zpart,
    wv, dv, rsum, tang, csend, crecv, keep, xsend, xrecv, zsend, zrecv,
    local, ag_recv, ag_zsend, ag_xsend, ag_csend,
    root_send, root_recv, cz_send, cz_recv, cp_send, cp_recv, cg_send, cg_recv,
    gc_send, gc_recv, gx_send, gx_recv, gz_send, gz_recv,
):
    rows = men_hbm.shape[0]
    width = women_hbm.shape[0]
    group = n_women * width
    n_chips = n_men // 2
    chunk = min(rows, 256)
    m = lax.axis_index("men")
    w = lax.axis_index("women")
    c = m // 2
    core = m % 2
    sib = c * 2 + (1 - core)

    def z_to(j):
        return lax.rem(w + j, n_women)

    def z_from(j):
        return lax.rem(w + n_women - j, n_women)

    def chip_to(k):
        if n_chips == 4:
            return (c // 2 + k // 2) % 2 * 2 + (c + k) % 2
        return lax.rem(c + k, n_chips)

    def chip_from(k):
        if n_chips == 4:
            return chip_to(k)
        return lax.rem(c + n_chips - k, n_chips)

    def copy(src, dst, send, recv, to_m, to_w):
        return pltpu.make_async_remote_copy(
            src_ref=src, dst_ref=dst, send_sem=send, recv_sem=recv,
            device_id=(to_m, to_w), device_id_type=MESH,
        )

    fetches = [
        pltpu.make_async_copy(src, dst, local.at[i])
        for i, (src, dst) in enumerate((
            (women_hbm, wbuf.at[m, w]), (root_hbm, rootbuf.at[w]),
            (wcount_hbm, wcountbuf.at[w]), (wcot_hbm, wcotbuf.at[w]),
            (men_hbm, men_ref), (count_hbm.at[w], count_ref), (cot_hbm.at[w], cot_ref),
        ))
    ]
    for fetch in fetches:
        fetch.start()

    barrier = pltpu.get_barrier_semaphore()
    loop(1, n_women, lambda j: pl.semaphore_signal(
        barrier, inc=1, device_id=(m, z_to(j)), device_id_type=MESH))
    loop(1, n_men, lambda j: pl.semaphore_signal(
        barrier, inc=1, device_id=(lax.rem(m + j, n_men), w), device_id_type=MESH))
    fetches[0].wait()
    pl.semaphore_wait(barrier, n_women + n_men - 2)

    def block_copy(at_m, at_w, send, to_m, to_w):
        return copy(wbuf.at[at_m, at_w], wbuf.at[at_m, at_w], send,
                    ag_recv.at[at_m, at_w], to_m, to_w)

    def z_copy(j):
        return block_copy(m, w, ag_zsend.at[j], m, z_to(j))

    def x_copy(k, j):
        return block_copy(m, z_from(j), ag_xsend.at[k, j], chip_to(k) * 2 + core, w)

    def c_copy(k, j):
        return block_copy(chip_from(k) * 2 + core, z_from(j), ag_csend.at[k, j], sib, w)

    def landed(at_m, at_w):
        block_copy(at_m, at_w, ag_zsend.at[0], sib, w).wait_recv()

    def vector_copies(j):
        return [copy(buf.at[w], buf.at[w], root_send.at[i, j], root_recv.at[i, j], m, z_to(j))
                for i, buf in enumerate((rootbuf, wcountbuf, wcotbuf))]

    def each(copies, act):
        for one in copies:
            getattr(one, act)()

    loop(1, n_women, lambda j: z_copy(j).start())
    loop(1, n_chips, lambda k: x_copy(n_chips - k, 0).start())
    c_copy(0, 0).start()
    for fetch in fetches[1:]:
        fetch.wait()
    loop(1, n_women, lambda j: each(vector_copies(j), "start"))

    def column(row):
        return jnp.broadcast_to(row, (128, rows)).T

    mass = column(count_ref[...].astype(F32))
    men_cot = column(cot_ref[...])
    men_t = men_ref[...].astype(F32).T.astype(BF16)
    rsum[...] = jnp.zeros_like(rsum)
    wv[...] = jnp.zeros_like(wv)

    def pass_on(j):
        landed(m, z_from(j))
        loop(1, n_chips, lambda k: x_copy(n_chips - k, j).start())
        c_copy(0, j).start()

    loop(1, n_women, pass_on)
    loop(1, n_women, lambda j: each(vector_copies(j), "wait_recv"))

    def spread(buf, out):
        for i in range(n_women):
            out[:, i * width:(i + 1) * width] = buf[i]

    spread(rootbuf, rootg)
    spread(wcountbuf, wcountg)
    spread(wcotbuf, wcotg)

    def lanes(values):
        total = values[:, :128]
        for i in range(1, group // 128):
            total = total + values[:, i * 128:(i + 1) * 128]
        return total

    def first(g):
        block = wbuf[g].reshape(group, 128)
        roots = rootg[pl.ds(g, 1), :]
        for r in range(0, rows, chunk):
            at = pl.ds(r, chunk)
            phi = lax.dot_general(men_ref[at, :], block, (((1,), (1,)), ((), ())),
                                  preferred_element_type=F32)
            k = jnp.exp2(phi * HALF_LOG2E)
            kmat[g, at, :] = k
            weighted = k * roots
            rsum[at, :] += lanes(weighted)
            wv[at, :] += jnp.dot(weighted.astype(BF16), block, preferred_element_type=F32)

    def all_landed(at_m):
        loop(0, n_women, lambda i: landed(at_m, i))

    def from_chip(k):
        at_m = chip_from(k) * 2 + core

        def forward(j):
            landed(at_m, z_from(j))
            c_copy(k, j).start()

        loop(0, n_women, forward)
        first(at_m)

    def from_sibling(k):
        at_m = chip_from(k) * 2 + (1 - core)
        all_landed(at_m)
        first(at_m)

    first(m)
    from_sibling(0)
    loop(1, n_chips, from_chip)
    loop(1, n_chips, from_sibling)

    row_mass = jnp.broadcast_to(jnp.sum(rsum[...], axis=1, keepdims=True), (rows, 128))
    men_disc = jnp.sqrt(row_mass * row_mass + 4.0 * mass)
    men_root = 2.0 * mass / (row_mass + men_disc)

    def wide(values):
        return jnp.concatenate([values] * (group // 128), axis=1)

    def second(g):
        total = jnp.zeros((8, group), F32)
        for r in range(0, rows, chunk):
            term = kmat[g, pl.ds(r, chunk), :] * wide(men_root[r:r + chunk])
            total = total + jnp.sum(term.reshape(chunk // 8, 8, group), axis=0)
        colp[g] = jnp.sum(total, axis=0, keepdims=True)

    def near(j):
        return lax.rem(m + j, n_men)

    def cp_copy(j):
        return copy(colp.at[near(j)], colrecv.at[j], cp_send.at[j], cp_recv.at[j], near(j), w)

    def cz_copy(j):
        return copy(zpart.at[0], zpart.at[j], cz_send.at[j], cz_recv.at[j], m, z_to(j))

    def cg_copy(j):
        return copy(gradg.at[m], gradg.at[m], cg_send.at[j], cg_recv.at[j], near(j), w)

    def for_owner(j):
        second(near(j))
        cp_copy(j).start()

    loop(1, n_men, for_owner)
    second(m)
    zpart[0] = colp[m]
    rsum[...] = jnp.zeros_like(rsum)
    dv[...] = jnp.zeros_like(dv)

    def add_p(j):
        cp_copy(j).wait_recv()
        zpart[0] += colrecv[j]

    loop(1, n_men, add_p)
    loop(1, n_women, lambda j: cz_copy(j).start())
    colp[m] = zpart[0]

    def add_z(j):
        cz_copy(j).wait_recv()
        colp[m] += zpart[j]

    loop(1, n_women, add_z)
    col_mass = colp[m]
    women_mass = wcountg[pl.ds(m, 1), :].astype(F32)
    women_disc = jnp.sqrt(col_mass * col_mass + 4.0 * women_mass)
    gradg[m] = -wcotg[pl.ds(m, 1), :] / women_disc
    loop(1, n_men, lambda j: cg_copy(j).start())

    def third(g):
        block = wbuf[g].reshape(group, 128)
        grads = gradg[g]
        for r in range(0, rows, chunk):
            at = pl.ds(r, chunk)
            weighted = kmat[g, at, :] * grads
            rsum[at, :] += lanes(weighted)
            dv[at, :] += jnp.dot(weighted.astype(BF16), block, preferred_element_type=F32)

    def third_from(j):
        cg_copy(j).wait_recv()
        third(lax.rem(m + n_men - j, n_men))

    third(m)
    loop(1, n_men, third_from)
    row_cot = jnp.broadcast_to(jnp.sum(rsum[...], axis=1, keepdims=True), (rows, 128))
    row_grad = -(men_cot + men_root * row_cot) / men_disc
    half_grad = 0.5 * row_grad
    half_root = 0.5 * men_root
    men_out[...] = half_grad * wv[...] + half_root * dv[...]

    def fourth(g):
        roots = rootg[pl.ds(g, 1), :]
        grads = gradg[g]
        for r in range(0, rows, chunk):
            at = pl.ds(r, chunk)
            scale = wide(half_grad[r:r + chunk]) * roots + wide(half_root[r:r + chunk]) * grads
            tang[at, :] = (kmat[g, at, :] * scale).astype(BF16)
        return jnp.dot(men_t, tang[...], preferred_element_type=F32).T

    def gc_copy(k):
        return copy(csend.at[k], crecv.at[k], gc_send.at[k], gc_recv.at[k], sib, w)

    def gx_copy(k, j):
        return copy(xsend.at[k, z_to(j)], xrecv.at[k, z_to(j)], gx_send.at[k, j],
                    gx_recv.at[k, j], chip_to(k) * 2 + core, w)

    def gz_copy(j):
        return copy(zsend.at[j], zrecv.at[j], gz_send.at[j], gz_recv.at[j], m, z_to(j))

    def chip_terms(k):
        csend[k] = fourth(chip_to(k) * 2 + (1 - core))
        gc_copy(k).start()
        keep[...] = fourth(chip_to(k) * 2 + core)
        gc_copy(k).wait_recv()

    def to_chip(k):
        chip_terms(k)
        xsend[k] = (keep[...] + crecv[k]).reshape(n_women, width, 128).astype(BF16)
        loop(1, n_women, lambda j: gx_copy(k, j).start())
        gx_copy(k, 0).start()

    loop(1, n_chips, lambda k: to_chip(n_chips - k))
    chip_terms(0)
    keep[...] += crecv[0]

    def part(j):
        return keep.at[pl.ds(pl.multiple_of(z_to(j) * width, width), width), :]

    def add_x(j):
        loop(1, n_chips, lambda k: gx_copy(k, j).wait_recv())
        total = part(j)[...]
        for k in range(1, n_chips):
            total = total + xrecv[k, z_to(j)].astype(F32)
        return total

    def along_z(j):
        zsend[j] = add_x(j).astype(BF16)
        gz_copy(j).start()

    loop(1, n_women, along_z)
    women_out[...] = add_x(0)

    def add_grad(j):
        gz_copy(j).wait_recv()
        women_out[...] += zrecv[j].astype(F32)

    loop(1, n_women, add_grad)

    def z_sends(j):
        z_copy(j).wait_send()
        each(vector_copies(j), "wait_send")
        cz_copy(j).wait_send()
        gz_copy(j).wait_send()

    loop(1, n_women, z_sends)
    loop(1, n_men, lambda j: cp_copy(j).wait_send())
    loop(1, n_men, lambda j: cg_copy(j).wait_send())
    loop(0, n_women, lambda j: loop(1, n_chips, lambda k: x_copy(k, j).wait_send()))
    loop(0, n_women, lambda j: loop(0, n_chips, lambda k: c_copy(k, j).wait_send()))
    loop(0, n_chips, lambda k: gc_copy(k).wait_send())
    loop(0, n_women, lambda j: loop(1, n_chips, lambda k: gx_copy(k, j).wait_send()))


def body(
    n_men, n_women,
    men_embed, women_embed, men_count, women_count, women_root, men_cotangent, women_cotangent
):
    rows, emb = men_embed.shape
    width = women_embed.shape[0]
    group = n_women * width
    n_chips = n_men // 2
    dma = pltpu.SemaphoreType.DMA
    vmem = pl.BlockSpec(memory_space=pltpu.VMEM)
    quarter = (n_men, width)
    return pl.pallas_call(
        functools.partial(kernel, n_men, n_women),
        out_shape=(
            jax.ShapeDtypeStruct((rows, emb), F32),
            jax.ShapeDtypeStruct((width, emb), F32),
        ),
        in_specs=[pl.BlockSpec(memory_space=pltpu.HBM)] * 7,
        out_specs=(vmem, vmem),
        scratch_shapes=[
            pltpu.VMEM((rows, emb), BF16),
            pltpu.VMEM((1, rows), jnp.int32),
            pltpu.VMEM((1, rows), F32),
            pltpu.VMEM((n_men, n_women, width, emb), BF16),
            pltpu.VMEM((n_men, rows, group), F32),
            pltpu.VMEM((n_women,) + quarter, F32),
            pltpu.VMEM((n_women,) + quarter, jnp.int32),
            pltpu.VMEM((n_women,) + quarter, F32),
            pltpu.VMEM((n_men, group), F32),
            pltpu.VMEM((n_men, group), jnp.int32),
            pltpu.VMEM((n_men, group), F32),
            pltpu.VMEM((n_men, 1, group), F32),
            pltpu.VMEM((n_men, 1, group), F32),
            pltpu.VMEM((n_men, 1, group), F32),
            pltpu.VMEM((n_women, 1, group), F32),
            pltpu.VMEM((rows, emb), F32),
            pltpu.VMEM((rows, emb), F32),
            pltpu.VMEM((rows, 128), F32),
            pltpu.VMEM((rows, group), BF16),
            pltpu.VMEM((n_chips, group, emb), F32),
            pltpu.VMEM((n_chips, group, emb), F32),
            pltpu.VMEM((group, emb), F32),
            pltpu.VMEM((n_chips, n_women, width, emb), BF16),
            pltpu.VMEM((n_chips, n_women, width, emb), BF16),
            pltpu.VMEM((n_women, width, emb), BF16),
            pltpu.VMEM((n_women, width, emb), BF16),
            dma((7,)),
            dma((n_men, n_women)),
            dma((n_women,)),
            dma((n_chips, n_women)),
            dma((n_chips, n_women)),
            dma((3, n_women)), dma((3, n_women)),
            dma((n_women,)), dma((n_women,)),
            dma((n_men,)), dma((n_men,)),
            dma((n_men,)), dma((n_men,)),
            dma((n_chips,)), dma((n_chips,)),
            dma((n_chips, n_women)), dma((n_chips, n_women)),
            dma((n_women,)), dma((n_women,)),
        ],
        compiler_params=pltpu.CompilerParams(
            collective_id=0, has_side_effects=True, vmem_limit_bytes=60 * 1024 * 1024,
        ),
        name="matching_backward",
    )(
        men_embed, women_embed,
        men_count.reshape(n_women, 1, rows), men_cotangent.reshape(n_women, 1, rows),
        women_root.reshape(quarter), women_count.reshape(quarter),
        women_cotangent.reshape(quarter),
    )


def solution(mesh):
    return jax.shard_map(
        functools.partial(body, mesh.shape["men"], mesh.shape["women"]),
        mesh=mesh,
        in_specs=(
            P(("men", "women"), None),
            P(("women", "men"), None),
            P("men"),
            P("women"),
            P("women"),
            P("men"),
            P("women"),
        ),
        out_specs=(P(("men", "women"), None), P(("women", "men"), None)),
        check_vma=False,
    )
```

```python
import functools
import math

import jax
import jax.numpy as jnp
from jax import lax
from jax.experimental import pallas as pl
from jax.experimental.pallas import tpu as pltpu
from jax.sharding import PartitionSpec as P

F32 = jnp.float32
BF16 = jnp.bfloat16
MESH = pl.DeviceIdType.MESH
HALF_LOG2E = 0.5 * math.log2(math.e)


def loop(start, stop, step_fn):
    if stop - start <= 8:
        for i in range(start, stop):
            step_fn(i)
    else:
        lax.fori_loop(start, stop, lambda i, _: (step_fn(i), 0)[1], 0)


def kernel(
    n_men, n_women,
    men_hbm, women_hbm, count_hbm, cot_hbm, root_hbm, wcount_hbm, wcot_hbm,
    men_out, women_out,
    men_ref, count_ref, cot_ref, wbuf, kmat, rootbuf, wcountbuf, wcotbuf,
    rootg, wcountg, wcotg, gradg, colp, colrecv, zpart,
    wv, dv, rsum, tang, csend, crecv, keep, xsend, xrecv, zsend, zrecv,
    local, ag_recv, ag_zsend, ag_xsend, ag_csend,
    root_send, root_recv, cz_send, cz_recv, cp_send, cp_recv, cg_send, cg_recv,
    gc_send, gc_recv, gx_send, gx_recv, gz_send, gz_recv,
):
    rows = men_hbm.shape[0]
    width = women_hbm.shape[0]
    group = n_women * width
    n_chips = n_men // 2
    chunk = min(rows, 512)
    m = lax.axis_index("men")
    w = lax.axis_index("women")
    c = m // 2
    core = m % 2
    sib = c * 2 + (1 - core)

    def z_to(j):
        return lax.rem(w + j, n_women)

    def z_from(j):
        return lax.rem(w + n_women - j, n_women)

    def chip_to(k):
        if n_chips == 4:
            return (c // 2 + k // 2) % 2 * 2 + (c + k) % 2
        return lax.rem(c + k, n_chips)

    def chip_from(k):
        if n_chips == 4:
            return chip_to(k)
        return lax.rem(c + n_chips - k, n_chips)

    def copy(src, dst, send, recv, to_m, to_w):
        return pltpu.make_async_remote_copy(
            src_ref=src, dst_ref=dst, send_sem=send, recv_sem=recv,
            device_id=(to_m, to_w), device_id_type=MESH,
        )

    fetches = [
        pltpu.make_async_copy(src, dst, local.at[i])
        for i, (src, dst) in enumerate((
            (women_hbm, wbuf.at[m, w]), (root_hbm, rootbuf.at[w]),
            (wcount_hbm, wcountbuf.at[w]), (wcot_hbm, wcotbuf.at[w]),
            (men_hbm, men_ref), (count_hbm.at[w], count_ref), (cot_hbm.at[w], cot_ref),
        ))
    ]
    for fetch in fetches:
        fetch.start()

    barrier = pltpu.get_barrier_semaphore()
    loop(1, n_women, lambda j: pl.semaphore_signal(
        barrier, inc=1, device_id=(m, z_to(j)), device_id_type=MESH))
    loop(1, n_men, lambda j: pl.semaphore_signal(
        barrier, inc=1, device_id=(lax.rem(m + j, n_men), w), device_id_type=MESH))
    fetches[0].wait()
    pl.semaphore_wait(barrier, n_women + n_men - 2)

    def block_copy(at_m, at_w, send, to_m, to_w):
        return copy(wbuf.at[at_m, at_w], wbuf.at[at_m, at_w], send,
                    ag_recv.at[at_m, at_w], to_m, to_w)

    def z_copy(j):
        return block_copy(m, w, ag_zsend.at[j], m, z_to(j))

    def x_copy(k, j):
        return block_copy(m, z_from(j), ag_xsend.at[k, j], chip_to(k) * 2 + core, w)

    def c_copy(k, j):
        return block_copy(chip_from(k) * 2 + core, z_from(j), ag_csend.at[k, j], sib, w)

    def landed(at_m, at_w):
        block_copy(at_m, at_w, ag_zsend.at[0], sib, w).wait_recv()

    def vector_copies(j):
        return [copy(buf.at[w], buf.at[w], root_send.at[i, j], root_recv.at[i, j], m, z_to(j))
                for i, buf in enumerate((rootbuf, wcountbuf, wcotbuf))]

    def each(copies, act):
        for one in copies:
            getattr(one, act)()

    loop(1, n_women, lambda j: z_copy(j).start())
    loop(1, n_chips, lambda k: x_copy(n_chips - k, 0).start())
    c_copy(0, 0).start()
    for fetch in fetches[1:]:
        fetch.wait()
    loop(1, n_women, lambda j: each(vector_copies(j), "start"))

    def column(row):
        return jnp.broadcast_to(row, (128, rows)).T

    mass = column(count_ref[...].astype(F32))
    men_cot = column(cot_ref[...])
    men_t = men_ref[...].astype(F32).T.astype(BF16)
    rsum[...] = jnp.zeros_like(rsum)
    wv[...] = jnp.zeros_like(wv)

    def pass_on(j):
        landed(m, z_from(j))
        loop(1, n_chips, lambda k: x_copy(n_chips - k, j).start())
        c_copy(0, j).start()

    loop(1, n_women, pass_on)
    loop(1, n_women, lambda j: each(vector_copies(j), "wait_recv"))

    def spread(buf, out):
        for i in range(n_women):
            out[:, i * width:(i + 1) * width] = buf[i]

    spread(rootbuf, rootg)
    spread(wcountbuf, wcountg)
    spread(wcotbuf, wcotg)

    def lanes(values):
        total = values[:, :128]
        for i in range(1, group // 128):
            total = total + values[:, i * 128:(i + 1) * 128]
        return total

    def first(g):
        block = wbuf[g].reshape(group, 128)
        roots = rootg[pl.ds(g, 1), :]
        for r in range(0, rows, chunk):
            at = pl.ds(r, chunk)
            phi = lax.dot_general(men_ref[at, :], block, (((1,), (1,)), ((), ())),
                                  preferred_element_type=F32)
            k = jnp.exp2(phi * HALF_LOG2E)
            kmat[g, at, :] = k
            weighted = k * roots
            rsum[at, :] += lanes(weighted)
            wv[at, :] += jnp.dot(weighted.astype(BF16), block, preferred_element_type=F32)

    def all_landed(at_m):
        loop(0, n_women, lambda i: landed(at_m, i))

    def from_chip(k):
        at_m = chip_from(k) * 2 + core

        def forward(j):
            landed(at_m, z_from(j))
            c_copy(k, j).start()

        loop(0, n_women, forward)
        first(at_m)

    def from_sibling(k):
        at_m = chip_from(k) * 2 + (1 - core)
        all_landed(at_m)
        first(at_m)

    first(m)
    from_sibling(0)
    loop(1, n_chips, from_chip)
    loop(1, n_chips, from_sibling)

    row_mass = jnp.broadcast_to(jnp.sum(rsum[...], axis=1, keepdims=True), (rows, 128))
    men_disc = jnp.sqrt(row_mass * row_mass + 4.0 * mass)
    men_root = 2.0 * mass / (row_mass + men_disc)

    def wide(values):
        return jnp.concatenate([values] * (group // 128), axis=1)

    def second(g):
        total = jnp.zeros((8, group), F32)
        for r in range(0, rows, chunk):
            term = kmat[g, pl.ds(r, chunk), :] * wide(men_root[r:r + chunk])
            total = total + jnp.sum(term.reshape(chunk // 8, 8, group), axis=0)
        colp[g] = jnp.sum(total, axis=0, keepdims=True)

    def near(j):
        return lax.rem(m + j, n_men)

    def cp_copy(j):
        return copy(colp.at[near(j)], colrecv.at[j], cp_send.at[j], cp_recv.at[j], near(j), w)

    def cz_copy(j):
        return copy(zpart.at[0], zpart.at[j], cz_send.at[j], cz_recv.at[j], m, z_to(j))

    def cg_copy(j):
        return copy(gradg.at[m], gradg.at[m], cg_send.at[j], cg_recv.at[j], near(j), w)

    def for_owner(j):
        second(near(j))
        cp_copy(j).start()

    loop(1, n_men, for_owner)
    second(m)
    zpart[0] = colp[m]
    rsum[...] = jnp.zeros_like(rsum)
    dv[...] = jnp.zeros_like(dv)

    def add_p(j):
        cp_copy(j).wait_recv()
        zpart[0] += colrecv[j]

    loop(1, n_men, add_p)
    loop(1, n_women, lambda j: cz_copy(j).start())
    colp[m] = zpart[0]

    def add_z(j):
        cz_copy(j).wait_recv()
        colp[m] += zpart[j]

    loop(1, n_women, add_z)
    col_mass = colp[m]
    women_mass = wcountg[pl.ds(m, 1), :].astype(F32)
    women_disc = jnp.sqrt(col_mass * col_mass + 4.0 * women_mass)
    gradg[m] = -wcotg[pl.ds(m, 1), :] / women_disc
    loop(1, n_men, lambda j: cg_copy(j).start())

    def third(g):
        block = wbuf[g].reshape(group, 128)
        grads = gradg[g]
        for r in range(0, rows, chunk):
            at = pl.ds(r, chunk)
            weighted = kmat[g, at, :] * grads
            rsum[at, :] += lanes(weighted)
            dv[at, :] += jnp.dot(weighted.astype(BF16), block, preferred_element_type=F32)

    def third_from(j):
        cg_copy(j).wait_recv()
        third(lax.rem(m + n_men - j, n_men))

    third(m)
    loop(1, n_men, third_from)
    row_cot = jnp.broadcast_to(jnp.sum(rsum[...], axis=1, keepdims=True), (rows, 128))
    row_grad = -(men_cot + men_root * row_cot) / men_disc
    half_grad = 0.5 * row_grad
    half_root = 0.5 * men_root
    men_out[...] = half_grad * wv[...] + half_root * dv[...]

    def fourth(g):
        roots = rootg[pl.ds(g, 1), :]
        grads = gradg[g]
        for r in range(0, rows, chunk):
            at = pl.ds(r, chunk)
            scale = wide(half_grad[r:r + chunk]) * roots + wide(half_root[r:r + chunk]) * grads
            tang[at, :] = (kmat[g, at, :] * scale).astype(BF16)
        return jnp.dot(men_t, tang[...], preferred_element_type=F32).T

    def gc_copy(k):
        return copy(csend.at[k], crecv.at[k], gc_send.at[k], gc_recv.at[k], sib, w)

    def gx_copy(k, j):
        return copy(xsend.at[k, z_to(j)], xrecv.at[k, z_to(j)], gx_send.at[k, j],
                    gx_recv.at[k, j], chip_to(k) * 2 + core, w)

    def gz_copy(j):
        return copy(zsend.at[j], zrecv.at[j], gz_send.at[j], gz_recv.at[j], m, z_to(j))

    def chip_terms(k):
        csend[k] = fourth(chip_to(k) * 2 + (1 - core))
        gc_copy(k).start()
        keep[...] = fourth(chip_to(k) * 2 + core)
        gc_copy(k).wait_recv()

    def to_chip(k):
        chip_terms(k)
        xsend[k] = (keep[...] + crecv[k]).reshape(n_women, width, 128).astype(BF16)
        loop(1, n_women, lambda j: gx_copy(k, j).start())
        gx_copy(k, 0).start()

    loop(1, n_chips, lambda k: to_chip(n_chips - k))
    chip_terms(0)
    keep[...] += crecv[0]

    def part(j):
        return keep.at[pl.ds(pl.multiple_of(z_to(j) * width, width), width), :]

    def add_x(j):
        loop(1, n_chips, lambda k: gx_copy(k, j).wait_recv())
        total = part(j)[...]
        for k in range(1, n_chips):
            total = total + xrecv[k, z_to(j)].astype(F32)
        return total

    def along_z(j):
        zsend[j] = add_x(j).astype(BF16)
        gz_copy(j).start()

    loop(1, n_women, along_z)
    women_out[...] = add_x(0)

    def add_grad(j):
        gz_copy(j).wait_recv()
        women_out[...] += zrecv[j].astype(F32)

    loop(1, n_women, add_grad)

    def z_sends(j):
        z_copy(j).wait_send()
        each(vector_copies(j), "wait_send")
        cz_copy(j).wait_send()
        gz_copy(j).wait_send()

    loop(1, n_women, z_sends)
    loop(1, n_men, lambda j: cp_copy(j).wait_send())
    loop(1, n_men, lambda j: cg_copy(j).wait_send())
    loop(0, n_women, lambda j: loop(1, n_chips, lambda k: x_copy(k, j).wait_send()))
    loop(0, n_women, lambda j: loop(0, n_chips, lambda k: c_copy(k, j).wait_send()))
    loop(0, n_chips, lambda k: gc_copy(k).wait_send())
    loop(0, n_women, lambda j: loop(1, n_chips, lambda k: gx_copy(k, j).wait_send()))


def body(
    n_men, n_women,
    men_embed, women_embed, men_count, women_count, women_root, men_cotangent, women_cotangent
):
    rows, emb = men_embed.shape
    width = women_embed.shape[0]
    group = n_women * width
    n_chips = n_men // 2
    dma = pltpu.SemaphoreType.DMA
    vmem = pl.BlockSpec(memory_space=pltpu.VMEM)
    quarter = (n_men, width)
    return pl.pallas_call(
        functools.partial(kernel, n_men, n_women),
        out_shape=(
            jax.ShapeDtypeStruct((rows, emb), F32),
            jax.ShapeDtypeStruct((width, emb), F32),
        ),
        in_specs=[pl.BlockSpec(memory_space=pltpu.HBM)] * 7,
        out_specs=(vmem, vmem),
        scratch_shapes=[
            pltpu.VMEM((rows, emb), BF16),
            pltpu.VMEM((1, rows), jnp.int32),
            pltpu.VMEM((1, rows), F32),
            pltpu.VMEM((n_men, n_women, width, emb), BF16),
            pltpu.VMEM((n_men, rows, group), F32),
            pltpu.VMEM((n_women,) + quarter, F32),
            pltpu.VMEM((n_women,) + quarter, jnp.int32),
            pltpu.VMEM((n_women,) + quarter, F32),
            pltpu.VMEM((n_men, group), F32),
            pltpu.VMEM((n_men, group), jnp.int32),
            pltpu.VMEM((n_men, group), F32),
            pltpu.VMEM((n_men, 1, group), F32),
            pltpu.VMEM((n_men, 1, group), F32),
            pltpu.VMEM((n_men, 1, group), F32),
            pltpu.VMEM((n_women, 1, group), F32),
            pltpu.VMEM((rows, emb), F32),
            pltpu.VMEM((rows, emb), F32),
            pltpu.VMEM((rows, 128), F32),
            pltpu.VMEM((rows, group), BF16),
            pltpu.VMEM((n_chips, group, emb), F32),
            pltpu.VMEM((n_chips, group, emb), F32),
            pltpu.VMEM((group, emb), F32),
            pltpu.VMEM((n_chips, n_women, width, emb), BF16),
            pltpu.VMEM((n_chips, n_women, width, emb), BF16),
            pltpu.VMEM((n_women, width, emb), BF16),
            pltpu.VMEM((n_women, width, emb), BF16),
            dma((7,)),
            dma((n_men, n_women)),
            dma((n_women,)),
            dma((n_chips, n_women)),
            dma((n_chips, n_women)),
            dma((3, n_women)), dma((3, n_women)),
            dma((n_women,)), dma((n_women,)),
            dma((n_men,)), dma((n_men,)),
            dma((n_men,)), dma((n_men,)),
            dma((n_chips,)), dma((n_chips,)),
            dma((n_chips, n_women)), dma((n_chips, n_women)),
            dma((n_women,)), dma((n_women,)),
        ],
        compiler_params=pltpu.CompilerParams(
            collective_id=0, has_side_effects=True, vmem_limit_bytes=60 * 1024 * 1024,
        ),
        name="matching_backward",
    )(
        men_embed, women_embed,
        men_count.reshape(n_women, 1, rows), men_cotangent.reshape(n_women, 1, rows),
        women_root.reshape(quarter), women_count.reshape(quarter),
        women_cotangent.reshape(quarter),
    )


def solution(mesh):
    return jax.shard_map(
        functools.partial(body, mesh.shape["men"], mesh.shape["women"]),
        mesh=mesh,
        in_specs=(
            P(("men", "women"), None),
            P(("women", "men"), None),
            P("men"),
            P("women"),
            P("women"),
            P("men"),
            P("women"),
        ),
        out_specs=(P(("men", "women"), None), P(("women", "men"), None)),
        check_vma=False,
    )
```
